256 devices in a mesh: section: 8 (over x, y_lo), expert: 32 (over z, y_hi, core).
Axes of the slice: x: 4, y: 4 (y_hi: 2, y_lo: 2; y = y_hi * 2 + y_lo), z: 8, core: 2. Of those that a mesh axis runs over, the one named last changes fastest.
Arguments:
- fwd_inputs: bfloat16 [8, 4096, 7168], P('section', 'expert'), may hold values from -6 to 6
- fwd_gates: float32 [8, 4096, 8], P('section', 'expert'), may hold values from 0.1 to 1
- fwd_routes: int32 [8, 4096, 8], P('section', 'expert'), may hold values from 0 to 255, as said below
- bwd_saved: bfloat16 [8, 512, 7168], P('section', 'expert'), may hold values from -6 to 6
- bwd_cotangents: bfloat16 [8, 4096, 7168], P('section', 'expert'), may hold values from -0.59765625 to 0.59765625
- bwd_gates: float32 [8, 4096, 8], P('section', 'expert'), may hold values from 0.1 to 1
- bwd_routes: int32 [8, 4096, 8], P('section', 'expert'), may hold values from 0 to 255, as said below
- w_gate: bfloat16 [8, 7168, 4096], P('section', None, 'expert'), may hold values from -0.0625 to 0.0625
- w_up: bfloat16 [8, 7168, 4096], P('section', None, 'expert'), may hold values from -0.0625 to 0.0625
- w_down: bfloat16 [8, 4096, 7168], P('section', 'expert'), may hold values from -0.125 to 0.125
Outputs:
- fwd_outputs: bfloat16 [8, 4096, 7168], P('section', 'expert')
- bwd_input_grads: bfloat16 [8, 4096, 7168], P('section', 'expert')
- bwd_gate_grads: float32 [8, 4096, 8], P('section', 'expert')
The draws below stay inside these ranges and needn't reach their ends.
Inputs may be any that keep to these rules, and one draw needn't show every extreme that they name: `fwd_routes`: each row names 8 different experts. In each aligned block of 128 rows of a section, each expert below 2 is named by at least half of 8 and at most 8 rows; for each such expert there is a section where every block has exactly 8. `bwd_routes`: as for fwd_routes.
All inputs are finite; a program needn't handle non-finite values.
Results may differ from the reference program's by a relative error of at most 0.008.
Values may be sent and summed in bfloat16 or wider, within the bound.
A program may use at most 128 MiB of HBM per device.

```python
import jax
import jax.numpy as jnp
from jax import lax

D = 7168
FF = 2048
EXPERTS = 256
TOP = 8
FLIGHT = 2
TOK_DEV = 128
CAP = 8
SECTIONS = 8
TOKENS = 4096
PIECES = 16
SHARD = 128
N_EXPERT = 32


def route_draw(key):
    per_section = TOKENS // TOK_DEV
    others_range = EXPERTS - FLIGHT
    keys = jax.random.split(key, 6)
    start = jax.random.randint(keys[0], (SECTIONS, per_section, TOK_DEV, 1), 0, others_range)
    stride_top = max((others_range - 1) // (TOP - 1), 1)
    stride = jax.random.randint(keys[1], (SECTIONS, per_section, TOK_DEV, 1), 1, stride_top + 1)
    offsets = jnp.arange(TOP, dtype=jnp.int32)[None, None, None, :]
    routes = FLIGHT + (start + offsets * stride) % others_range
    counts = jax.random.randint(keys[2], (SECTIONS, per_section, FLIGHT), CAP // 2, CAP + 1)
    full_section = jax.random.randint(keys[3], (FLIGHT,), 0, SECTIONS)
    section_ids = jnp.arange(SECTIONS, dtype=jnp.int32)[:, None, None]
    counts = jnp.where(section_ids == full_section[None, None, :], CAP, counts)
    scores = jax.random.randint(keys[4], (SECTIONS, per_section, FLIGHT, TOK_DEV), 0, 2 ** 20)
    scores = scores * TOK_DEV + jnp.arange(TOK_DEV, dtype=jnp.int32)
    ranks = jnp.argsort(jnp.argsort(scores, axis=3, stable=True), axis=3, stable=True)
    member = ranks < counts[:, :, :, None]
    first = jax.random.randint(keys[5], (SECTIONS, per_section, TOK_DEV), 0, TOP)
    places = jnp.arange(TOP, dtype=jnp.int32)
    for expert_index in range(FLIGHT):
        target = (first + expert_index) % TOP
        put = member[:, :, expert_index, :, None] & (places[None, None, None, :] == target[:, :, :, None])
        routes = jnp.where(put, expert_index, routes)
    return routes.reshape(SECTIONS, TOKENS, TOP).astype(jnp.int32)


def draw_fwd_routes(key, part):
    key = jax.random.fold_in(key, 11)
    return route_draw(key)


def draw_bwd_routes(key, part):
    key = jax.random.fold_in(key, 12)
    return route_draw(key)


def block_scale(key, shape, cuts, least, largest):
    loudness = 1.0
    for dim, shards_of in cuts:
        steps = jax.random.uniform(jax.random.fold_in(jax.random.fold_in(key, 6), dim), (shards_of,), jnp.float32, least / len(cuts), largest / len(cuts))
        loudness = loudness * jnp.repeat(jnp.exp(steps), shape[dim] // shards_of).reshape((-1,) + (1,) * (len(shape) - 1 - dim))
    return loudness


def gaussian(stream_key, dims, deviation, reach, cuts=(), held_as=jnp.bfloat16):
    values = deviation * jax.random.normal(stream_key, dims, jnp.float32)
    if cuts:
        values = values * block_scale(stream_key, dims, cuts, -0.22, 0.18)
    return jnp.clip(values, -reach, reach).astype(held_as)


def setup_inputs(seed: int = 0) -> dict:
    key_list = jax.random.split(jax.random.key(seed), 11)
    fwd_inputs = gaussian(key_list[0], (SECTIONS, TOKENS, D), 1.0, 6.0, ((0, 8), (1, 32)))
    fwd_gates = jnp.clip(0.1 + 0.9 * jax.random.uniform(key_list[1], (SECTIONS, TOKENS, TOP), jnp.float32) ** block_scale(key_list[1], (SECTIONS, TOKENS, TOP), ((0, 8), (1, 32)), -0.2, 0.2), 0.1, 1.0)
    fwd_routes = draw_fwd_routes(jax.random.fold_in(key_list[10], 71), 0)
    bwd_saved = gaussian(key_list[3], (SECTIONS, N_EXPERT * FLIGHT * CAP, D), 1.0, 6.0, ((0, 8), (1, 32)))
    bwd_cotangents = gaussian(key_list[4], (SECTIONS, TOKENS, D), 0.1, 0.59765625, ((0, 8), (1, 32)))
    bwd_gates = jnp.clip(0.1 + 0.9 * jax.random.uniform(key_list[5], (SECTIONS, TOKENS, TOP), jnp.float32) ** block_scale(key_list[5], (SECTIONS, TOKENS, TOP), ((0, 8), (1, 32)), -0.2, 0.2), 0.1, 1.0)
    bwd_routes = draw_bwd_routes(jax.random.fold_in(key_list[10], 71), 0)
    w_gate = gaussian(key_list[7], (SECTIONS, D, FLIGHT * FF), D ** -0.5, 0.0625, ((0, 8), (2, 32)))
    w_up = gaussian(key_list[8], (SECTIONS, D, FLIGHT * FF), D ** -0.5, 0.0625, ((0, 8), (2, 32)))
    w_down = gaussian(key_list[9], (SECTIONS, FLIGHT * FF, D), FF ** -0.5, 0.125, ((0, 8), (1, 32)))
    return {"fwd_inputs": fwd_inputs, "fwd_gates": fwd_gates, "fwd_routes": fwd_routes, "bwd_saved": bwd_saved, "bwd_cotangents": bwd_cotangents, "bwd_gates": bwd_gates, "bwd_routes": bwd_routes, "w_gate": w_gate, "w_up": w_up, "w_down": w_down}


def tables(routes, gates):
    expert_ids = jnp.arange(FLIGHT, dtype=jnp.int32)
    route_hits = routes[:, :, None, :] == expert_ids[None, None, :, None]
    member = jnp.sum(route_hits.astype(jnp.int32), axis=3)
    position = jnp.cumsum(member, axis=1).astype(jnp.int32) - 1
    slot_ids = jnp.arange(CAP, dtype=jnp.int32)
    onehot = (member[:, None, :, :] == 1) & (position[:, None, :, :] == slot_ids[None, :, None, None])
    onehot = jnp.transpose(onehot, (0, 3, 1, 2)).astype(jnp.float32)
    weight = jnp.sum(jnp.where(route_hits, gates[:, :, None, :], jnp.zeros_like(gates)[:, :, None, :]), axis=3)
    return onehot, route_hits, weight


def pack_slots(onehot, tokens):
    packed = jnp.einsum('bjct,btd->jbcd', onehot, tokens.astype(jnp.float32), precision=lax.Precision.HIGHEST)
    return packed.astype(jnp.bfloat16).reshape(FLIGHT, -1, D)


def shard_sum(terms):
    rounded = lax.optimization_barrier(terms.astype(jnp.bfloat16))
    return jnp.sum(rounded.astype(jnp.float32), axis=0)


def forward_rows(row_block, gate_cols, up_cols, down_rows):
    gate_pre = jnp.dot(row_block, gate_cols, preferred_element_type=jnp.float32)
    up_pre = jnp.dot(row_block, up_cols, preferred_element_type=jnp.float32)
    hidden = (jax.nn.silu(gate_pre) * up_pre).astype(jnp.bfloat16)
    pieces = jnp.einsum('rgh,ghd->grd', hidden.reshape(-1, PIECES, SHARD).astype(jnp.float32),
                        down_rows.reshape(PIECES, SHARD, D).astype(jnp.float32))
    return shard_sum(pieces)


def backward_rows(row_block, cot_block, gate_cols, up_cols, down_rows):
    gate_pre = jnp.dot(row_block, gate_cols, preferred_element_type=jnp.float32)
    up_pre = jnp.dot(row_block, up_cols, preferred_element_type=jnp.float32)
    sigmoid = jax.nn.sigmoid(gate_pre)
    hidden = (jax.nn.silu(gate_pre) * up_pre).astype(jnp.bfloat16)
    back_hidden = jnp.dot(cot_block, down_rows.T, preferred_element_type=jnp.float32)
    gate_terms = jnp.sum((back_hidden * hidden.astype(jnp.float32)).reshape(-1, PIECES, SHARD), axis=2)
    gate_slot = shard_sum(gate_terms.T)
    grad_gate = (back_hidden * up_pre * sigmoid * (1.0 + gate_pre * (1.0 - sigmoid))).astype(jnp.bfloat16)
    grad_up = (back_hidden * jax.nn.silu(gate_pre)).astype(jnp.bfloat16)
    terms = jnp.einsum('rgh,ghd->grd', grad_gate.reshape(-1, PIECES, SHARD).astype(jnp.float32),
                       gate_cols.T.reshape(PIECES, SHARD, D).astype(jnp.float32))
    terms = terms + jnp.einsum('rgh,ghd->grd', grad_up.reshape(-1, PIECES, SHARD).astype(jnp.float32),
                               up_cols.T.reshape(PIECES, SHARD, D).astype(jnp.float32))
    return shard_sum(terms), gate_slot


def reference(fwd_inputs, fwd_gates, fwd_routes, bwd_saved, bwd_cotangents, bwd_gates, bwd_routes, w_gate, w_up, w_down):
    blocks = TOKENS // TOK_DEV
    arrived_all = jnp.roll(fwd_inputs, 1, axis=0)
    incoming_all = jnp.roll(bwd_cotangents, -1, axis=0)
    fwd_list = []
    grad_list = []
    gate_list = []
    for section_index in range(SECTIONS):
        onehot, route_hits, weight = tables(fwd_routes[section_index].reshape(blocks, TOK_DEV, TOP),
                                            fwd_gates[section_index].reshape(blocks, TOK_DEV, TOP))
        packed = pack_slots(onehot, arrived_all[section_index].reshape(blocks, TOK_DEV, D))
        outputs = []
        for expert_index in range(FLIGHT):
            lower = expert_index * FF
            outputs.append(forward_rows(packed[expert_index], w_gate[section_index][:, lower:lower + FF],
                                        w_up[section_index][:, lower:lower + FF], w_down[section_index][lower:lower + FF, :]))
        expert_out = jnp.stack(outputs).reshape(FLIGHT, blocks, CAP, D)
        combined = jnp.einsum('bjct,btj,jbcd->btd', onehot, weight, expert_out, precision=lax.Precision.HIGHEST)
        fwd_list.append(combined.astype(jnp.bfloat16).reshape(TOKENS, D))

        onehot, route_hits, weight = tables(bwd_routes[section_index].reshape(blocks, TOK_DEV, TOP),
                                            bwd_gates[section_index].reshape(blocks, TOK_DEV, TOP))
        packed_x = jnp.transpose(bwd_saved[section_index].reshape(blocks, FLIGHT, CAP, D), (1, 0, 2, 3)).reshape(FLIGHT, -1, D)
        packed_g = pack_slots(onehot, incoming_all[section_index].reshape(blocks, TOK_DEV, D))
        input_slots = []
        gate_slots = []
        for expert_index in range(FLIGHT):
            lower = expert_index * FF
            input_slot, gate_slot = backward_rows(packed_x[expert_index], packed_g[expert_index],
                                                  w_gate[section_index][:, lower:lower + FF],
                                                  w_up[section_index][:, lower:lower + FF],
                                                  w_down[section_index][lower:lower + FF, :])
            input_slots.append(input_slot)
            gate_slots.append(gate_slot)
        input_slot = jnp.stack(input_slots).reshape(FLIGHT, blocks, CAP, D)
        gate_slot = jnp.stack(gate_slots).reshape(FLIGHT, blocks, CAP)
        grads = jnp.einsum('bjct,btj,jbcd->btd', onehot, weight, input_slot, precision=lax.Precision.HIGHEST)
        grad_list.append(grads.astype(jnp.bfloat16).reshape(TOKENS, D))
        slot_values = jnp.einsum('bjct,jbc->btj', onehot, gate_slot, precision=lax.Precision.HIGHEST)
        gate_grads = jnp.einsum('btjk,btj->btk', route_hits.astype(jnp.float32), slot_values, precision=lax.Precision.HIGHEST)
        gate_list.append(gate_grads.reshape(TOKENS, TOP))
    return jnp.stack(fwd_list), jnp.stack(grad_list), jnp.stack(gate_list)
```

```python
import jax
import jax.numpy as jnp
from jax import lax
from jax.sharding import PartitionSpec as P

FLIGHT = 2
CAP = 8


def shifted(block, axis, distance):
    devices = range(lax.axis_size(axis))
    route = [((i - distance) % len(devices), i) for i in devices]
    return lax.ppermute(block, axis, route)


def tables(routes, gates):
    expert_ids = jnp.arange(FLIGHT, dtype=jnp.int32)
    route_hits = routes[:, None, :] == expert_ids[None, :, None]
    member = jnp.sum(route_hits.astype(jnp.int32), axis=2)
    position = jnp.cumsum(member, axis=0) - 1
    slot_ids = jnp.arange(CAP, dtype=jnp.int32)
    onehot = (member[None, :, :] == 1) & (position[None, :, :] == slot_ids[:, None, None])
    onehot = jnp.transpose(onehot, (2, 0, 1)).astype(jnp.float32)
    weight = jnp.sum(
        jnp.where(route_hits, gates[:, None, :], jnp.zeros_like(gates)[:, None, :]), axis=2
    )
    return (onehot, route_hits, weight)


def pack_slots(onehot, tokens):
    packed = jnp.einsum(
        "jct,td->jcd", onehot.astype(jnp.bfloat16), tokens, preferred_element_type=jnp.float32
    )
    return packed.astype(jnp.bfloat16)


def combine(onehot, weight, slot_values):
    return jnp.einsum(
        "jct,tj,jcd->td", onehot, weight, slot_values, precision=lax.Precision.HIGHEST
    )


def forward_rows(row_block, gate_cols, up_cols, down_rows):
    gate_pre = jnp.dot(row_block, gate_cols, preferred_element_type=jnp.float32)
    up_pre = jnp.dot(row_block, up_cols, preferred_element_type=jnp.float32)
    hidden = (jax.nn.silu(gate_pre) * up_pre).astype(jnp.bfloat16)
    return jnp.dot(hidden, down_rows, preferred_element_type=jnp.float32)


def backward_rows(row_block, cot_block, gate_cols, up_cols, down_rows):
    gate_pre = jnp.dot(row_block, gate_cols, preferred_element_type=jnp.float32)
    up_pre = jnp.dot(row_block, up_cols, preferred_element_type=jnp.float32)
    sigmoid = jax.nn.sigmoid(gate_pre)
    hidden = (jax.nn.silu(gate_pre) * up_pre).astype(jnp.bfloat16)
    contract = (((1,), (1,)), ((), ()))
    back_hidden = lax.dot_general(
        cot_block, down_rows, contract, preferred_element_type=jnp.float32
    )
    gate_term = jnp.sum(back_hidden * hidden.astype(jnp.float32), axis=1)
    grad_gate = (back_hidden * up_pre * sigmoid * (1.0 + gate_pre * (1.0 - sigmoid))).astype(
        jnp.bfloat16
    )
    grad_up = (back_hidden * jax.nn.silu(gate_pre)).astype(jnp.bfloat16)
    input_term = lax.dot_general(grad_gate, gate_cols, contract, preferred_element_type=jnp.float32)
    input_term = input_term + lax.dot_general(
        grad_up, up_cols, contract, preferred_element_type=jnp.float32
    )
    return (input_term, gate_term)


def body(
    fwd_inputs,
    fwd_gates,
    fwd_routes,
    bwd_saved,
    bwd_cotangents,
    bwd_gates,
    bwd_routes,
    w_gate,
    w_up,
    w_down,
):
    device_count = lax.axis_size("expert")
    group_size = device_count // FLIGHT
    model_width = fwd_inputs.shape[2]
    gate_cols = w_gate[0]
    up_cols = w_up[0]
    down_rows = w_down[0]
    onehot_fwd, hits_fwd, weight_fwd = tables(fwd_routes[0], fwd_gates[0])
    onehot_bwd, hits_bwd, weight_bwd = tables(bwd_routes[0], bwd_gates[0])
    onehot_next = shifted(onehot_fwd.astype(jnp.bfloat16), "section", -1)
    onehot_previous = shifted(onehot_bwd.astype(jnp.bfloat16), "section", 1)
    packed_fwd = shifted(pack_slots(onehot_next, fwd_inputs[0]), "section", 1)
    packed_g = shifted(pack_slots(onehot_previous, bwd_cotangents[0]), "section", -1)
    received = lax.all_to_all(
        jnp.repeat(packed_fwd, group_size, axis=0),
        "expert",
        split_axis=0,
        concat_axis=0,
        tiled=True,
    )
    partial_value = forward_rows(received.reshape(-1, model_width), gate_cols, up_cols, down_rows)
    partial_value = partial_value.astype(jnp.bfloat16).reshape(device_count, CAP, model_width)
    returned = lax.all_to_all(partial_value, "expert", split_axis=0, concat_axis=0, tiled=True)
    expert_out = jnp.sum(
        returned.reshape(FLIGHT, group_size, CAP, model_width).astype(jnp.float32), axis=1
    )
    fwd_outputs = combine(onehot_fwd, weight_fwd, expert_out).astype(jnp.bfloat16)
    packed_x = bwd_saved[0].reshape(FLIGHT, CAP, model_width)
    recv_x, recv_g = (
        lax.all_to_all(
            jnp.repeat(packed_x, group_size, axis=0),
            "expert",
            split_axis=0,
            concat_axis=0,
            tiled=True,
        ),
        lax.all_to_all(
            jnp.repeat(packed_g, group_size, axis=0),
            "expert",
            split_axis=0,
            concat_axis=0,
            tiled=True,
        ),
    )
    input_term, gate_term = backward_rows(
        recv_x.reshape(-1, model_width),
        recv_g.reshape(-1, model_width),
        gate_cols,
        up_cols,
        down_rows,
    )
    input_term = input_term.astype(jnp.bfloat16).reshape(device_count, CAP, model_width)
    gate_term = gate_term.astype(jnp.bfloat16).reshape(device_count, CAP)
    back_input, back_gate = (
        lax.all_to_all(input_term, "expert", split_axis=0, concat_axis=0, tiled=True),
        lax.all_to_all(gate_term, "expert", split_axis=0, concat_axis=0, tiled=True),
    )
    input_slot = jnp.sum(
        back_input.reshape(FLIGHT, group_size, CAP, model_width).astype(jnp.float32), axis=1
    )
    gate_slot = jnp.sum(back_gate.reshape(FLIGHT, group_size, CAP).astype(jnp.float32), axis=1)
    bwd_input_grads = combine(onehot_bwd, weight_bwd, input_slot).astype(jnp.bfloat16)
    slot_values = jnp.einsum("jct,jc->tj", onehot_bwd, gate_slot, precision=lax.Precision.HIGHEST)
    bwd_gate_grads = jnp.einsum(
        "tjk,tj->tk", hits_bwd.astype(jnp.float32), slot_values, precision=lax.Precision.HIGHEST
    )
    return (fwd_outputs[None], bwd_input_grads[None], bwd_gate_grads[None])


def solution(mesh):
    placed = (
        P("section", "expert", None),
        P("section", "expert", None),
        P("section", "expert", None),
        P("section", "expert", None),
        P("section", "expert", None),
        P("section", "expert", None),
        P("section", "expert", None),
        P("section", None, "expert"),
        P("section", None, "expert"),
        P("section", "expert", None),
    )
    return jax.shard_map(
        body,
        mesh=mesh,
        in_specs=placed,
        out_specs=(
            P("section", "expert", None),
            P("section", "expert", None),
            P("section", "expert", None),
        ),
        check_vma=False,
    )
```
